32 devices in a mesh: tm: 4 (over x, core), space: 8 (over z, y).
Axes of the slice: x: 2, y: 2, z: 4, core: 2. Of those that a mesh axis runs over, the one named last changes fastest.
Arguments:
- queries: bfloat16 [4, 4, 8, 32, 1536], P('tm', None, 'space'), may hold values from -30 to 30
- key_states: bfloat16 [4, 4, 8, 32, 1536], P('tm', None, 'space'), may hold values from -30 to 30, as said below
- value_states: bfloat16 [4, 4, 8, 32, 1536], P('tm', None, 'space'), may hold values from -6 to 6
- conv_weight: float32 [3, 3, 3, 1536], replicated, may hold values from -0.3125 to 0.3125
Outputs:
- mixed: bfloat16 [4, 4, 8, 32, 1536], P('tm', None, 'space')
The draws below stay inside these ranges and needn't reach their ends.
Inputs may be any that keep to these rules, and one draw needn't show every extreme that they name: `key_states`: entries are real-valued keys.
All inputs are finite; a program needn't handle non-finite values.
Results may differ from the reference program's by a relative error of at most 0.0088.
Values may be sent and summed in bfloat16 or wider, within the bound.
A program may use at most 192 MiB of HBM per device.

```python
import jax
import jax.numpy as jnp
from jax import lax

HEADS = 24
HEAD_DIM = 64
D = 1536
FRAMES = 4
ROWS_DEV = 1
COLUMNS = 32
AGENT_DEV = 4
GROUPS = 4
ROWS = 8
AGENTS = 32
N_SPACE = 8


def draw_queries(key, part):
    region_key, noise_key = jax.random.split(jax.random.fold_in(key, 11))
    region = 0.5 * jax.random.normal(region_key, (GROUPS, AGENTS, D), jnp.float32)
    shape = (GROUPS, FRAMES, ROWS, COLUMNS, D)
    noise = 4.0 * jax.random.normal(noise_key, shape, jnp.float32)
    spread = region.reshape(GROUPS, 1, ROWS // ROWS_DEV, 1, AGENT_DEV, 1, D)
    spread = jnp.broadcast_to(spread, (GROUPS, FRAMES, ROWS // ROWS_DEV, ROWS_DEV, AGENT_DEV, COLUMNS // AGENT_DEV, D)).reshape(shape)
    return jnp.clip(spread + noise, -30.0, 30.0).astype(jnp.bfloat16)


def draw_key_states(key, part):
    noise_key = jax.random.fold_in(key, 13)
    shape = (GROUPS, FRAMES, ROWS, COLUMNS, D)
    states = 5.0 * jax.random.normal(noise_key, shape, jnp.float32)
    return jnp.clip(states, -30.0, 30.0).astype(jnp.bfloat16)


def shard_levels(rng, shape, cuts, smallest, top_value):
    def one(position, shards_of):
        draws = jax.random.uniform(jax.random.fold_in(jax.random.fold_in(rng, 6), position), (shards_of,), jnp.float32, smallest / len(cuts), top_value / len(cuts))
        return jnp.repeat(jnp.exp(draws), shape[position] // shards_of).reshape((-1,) + (1,) * (len(shape) - position - 1))

    factor_of = one(*cuts[0])
    for cut in cuts[1:]:
        factor_of = factor_of * one(*cut)
    return factor_of


def scatter_about(rng, shape, scale, reach, shards=(), held_as=jnp.bfloat16):
    drawn = jax.random.normal(rng, shape, jnp.float32) * scale
    if len(shards) > 0:
        drawn = shard_levels(rng, shape, shards, -0.22, 0.18) * drawn
    return jnp.clip(drawn, min=-reach, max=reach).astype(held_as)


def setup_inputs(seed: int = 0) -> dict:
    splits = jax.random.split(jax.random.key(seed), 5)
    return {
        "queries": draw_queries(jax.random.fold_in(splits[4], 71), 0),
        "key_states": draw_key_states(jax.random.fold_in(splits[4], 71), 0),
        "value_states": scatter_about(splits[2], (GROUPS, FRAMES, ROWS, COLUMNS, D), 1.0, 6.0, ((0, 4), (2, 8))),
        "conv_weight": scatter_about(splits[3], (3, 3, 3, D), 432 ** -0.5, 0.3125, (), jnp.float32),
    }


def mix_local(window, conv_weight):
    shape = (window.shape[0] - 2, window.shape[1] - 2, window.shape[2] - 2, window.shape[3])
    total = jnp.zeros(shape, jnp.float32)
    for time_off in range(3):
        for row_off in range(3):
            for col_off in range(3):
                piece = window[time_off:time_off + shape[0], row_off:row_off + shape[1], col_off:col_off + shape[2]]
                total = total + piece.astype(jnp.float32) * conv_weight[time_off, row_off, col_off]
    return total


def head_pass(inputs):
    query_head, key_head, value_head, agent_head = inputs
    inv_root = HEAD_DIM ** -0.5
    scores = jnp.dot(agent_head, key_head.T, preferred_element_type=jnp.float32) * inv_root
    weights = jnp.exp(scores - jnp.max(scores, axis=1, keepdims=True))
    totals = jnp.sum(weights, axis=1, keepdims=True)
    agent_values = (jnp.dot(weights.astype(jnp.bfloat16), value_head, preferred_element_type=jnp.float32) / totals).astype(jnp.bfloat16)
    query_scores = jnp.dot(query_head, agent_head.T, preferred_element_type=jnp.float32) * inv_root
    probs = jax.nn.softmax(query_scores, axis=1).astype(jnp.bfloat16)
    return jnp.dot(probs, agent_values, preferred_element_type=jnp.float32)


def split_heads(array, count):
    return array.reshape(count, HEADS, HEAD_DIM).transpose(1, 0, 2)


def reference(queries, key_states, value_states, conv_weight):
    timed = jnp.pad(value_states.reshape(GROUPS * FRAMES, ROWS, COLUMNS, D), ((1, 1), (0, 0), (0, 0), (0, 0)))

    def group_pass(inputs):
        group_query, group_key, group_value, group_index = inputs
        tokens = FRAMES * ROWS * COLUMNS
        pooled = jnp.mean(group_query.reshape(FRAMES, N_SPACE, ROWS_DEV, AGENT_DEV, COLUMNS // AGENT_DEV, D), axis=(0, 2, 4), dtype=jnp.float32)
        agents = pooled.reshape(AGENTS, D).astype(jnp.bfloat16)
        heads_out = lax.map(head_pass, (split_heads(group_query, tokens), split_heads(group_key, tokens), split_heads(group_value, tokens), split_heads(agents, AGENTS)))
        attended = heads_out.transpose(1, 0, 2).reshape(FRAMES, ROWS, COLUMNS, D)
        frames_cut = lax.dynamic_slice_in_dim(timed, group_index * FRAMES, FRAMES + 2, 0)
        window = jnp.pad(frames_cut, ((0, 0), (1, 1), (1, 1), (0, 0)))
        local_mix = mix_local(window, conv_weight)
        return (attended + local_mix).astype(jnp.bfloat16)

    return lax.map(group_pass, (queries, key_states, value_states, jnp.arange(GROUPS, dtype=jnp.int32)))
```

```python
import functools
import math

import jax
import jax.numpy as jnp
from jax import lax
from jax.experimental import pallas as pl
from jax.experimental.pallas import tpu as pltpu
from jax.sharding import PartitionSpec as P

HEADS = 24
HEAD_DIM = 64
D = 1536
FRAMES = 4
ROWS_DEV = 1
COLUMNS = 32
AGENT_DEV = 4
MESH = pl.DeviceIdType.MESH


def extended(cells, sides, width):
    for axis, dim in sides:
        count = lax.axis_size(axis)
        ends = count - 1
        head = lax.slice_in_dim(cells, 0, width, axis=dim)
        tail = lax.slice_in_dim(cells, cells.shape[dim] - width, cells.shape[dim], axis=dim)
        cells = jnp.concatenate(
            [
                lax.ppermute(tail, axis, [(i, (i + 1) % count) for i in range(ends)]),
                cells,
                lax.ppermute(head, axis, [((i + 1) % count, i) for i in range(ends)]),
            ],
            axis=dim,
        )
    return cells


def merged_2(part, axis, combine):
    gathered = jax.tree.map(lambda a: lax.all_gather(a, axis), part)

    def take(source):
        return jax.tree.map(lambda a: lax.dynamic_index_in_dim(a, source, 0, False), gathered)

    return lax.fori_loop(
        1, lax.axis_size(axis), lambda source, state: combine(state, take(source)), take(0)
    )


def mix_local(window, conv_weight):
    shape = (window.shape[0] - 2, window.shape[1] - 2, window.shape[2] - 2, window.shape[3])
    total = jnp.zeros(shape, jnp.float32)
    for time_off in range(3):
        for row_off in range(3):
            for col_off in range(3):
                piece = window[
                    time_off : time_off + shape[0],
                    row_off : row_off + shape[1],
                    col_off : col_off + shape[2],
                ]
                total = total + piece.astype(jnp.float32) * conv_weight[time_off, row_off, col_off]
    return total


def pair_merge(first, second):
    peak = jnp.maximum(first[0], second[0])
    left = jnp.exp(first[0] - peak)
    right = jnp.exp(second[0] - peak)
    return (
        peak,
        first[1] * left + second[1] * right,
        first[2] * left[..., None] + second[2] * right[..., None],
    )


def on_device(queries, key_states, value_states, conv_weight):
    tokens = FRAMES * ROWS_DEV * COLUMNS
    inv_root = HEAD_DIM ** (-0.5)
    per_block = math.gcd(HEADS, 8)
    blocks = HEADS // per_block
    padded = extended(value_states, (("tm", 1), ("space", 2)), 1)
    window = jnp.pad(padded[0], ((0, 0), (0, 0), (1, 1), (0, 0)))
    pooled = jnp.mean(
        queries.reshape(FRAMES, ROWS_DEV, AGENT_DEV, COLUMNS // AGENT_DEV, D),
        axis=(0, 1, 3),
        dtype=jnp.float32,
    )
    agents = lax.all_gather(pooled.astype(jnp.bfloat16), "space", axis=0, tiled=True)
    count = agents.shape[0]
    agent_heads = agents.reshape(count, HEADS, HEAD_DIM)
    query_heads = queries.reshape(tokens, HEADS, HEAD_DIM)
    key_heads = key_states.reshape(tokens, HEADS, HEAD_DIM)
    value_heads = value_states.reshape(tokens, HEADS, HEAD_DIM)

    def agent_block(index):
        start = index * per_block
        agent_part = lax.dynamic_slice_in_dim(agent_heads, start, per_block, 1)
        key_part = lax.dynamic_slice_in_dim(key_heads, start, per_block, 1)
        value_part = lax.dynamic_slice_in_dim(value_heads, start, per_block, 1)
        scores = (
            jnp.einsum("ahd,nhd->ahn", agent_part, key_part, preferred_element_type=jnp.float32)
            * inv_root
        )
        block_peak = jnp.max(scores, axis=2)
        weights = jnp.exp(scores - block_peak[..., None])
        block_total = jnp.sum(weights, axis=2)
        block_acc = jnp.einsum(
            "ahn,nhd->ahd",
            weights.astype(jnp.bfloat16),
            value_part,
            preferred_element_type=jnp.float32,
        )
        return (block_peak, block_total, block_acc)

    peaks, totals, accs = lax.map(agent_block, jnp.arange(blocks, dtype=jnp.int32))
    local_peak = peaks.transpose(1, 0, 2).reshape(count, HEADS)
    local_total = totals.transpose(1, 0, 2).reshape(count, HEADS)
    local_acc = accs.transpose(1, 0, 2, 3).reshape(count, HEADS, HEAD_DIM)
    merged = merged_2((local_peak, local_total, local_acc), "space", pair_merge)
    agent_values = (merged[2] / merged[1][..., None]).astype(jnp.bfloat16)

    def query_block(index):
        start = index * per_block
        query_part = lax.dynamic_slice_in_dim(query_heads, start, per_block, 1)
        agent_part = lax.dynamic_slice_in_dim(agent_heads, start, per_block, 1)
        values_part = lax.dynamic_slice_in_dim(agent_values, start, per_block, 1)
        query_scores = (
            jnp.einsum("nhd,ahd->hna", query_part, agent_part, preferred_element_type=jnp.float32)
            * inv_root
        )
        probs = jax.nn.softmax(query_scores, axis=-1).astype(jnp.bfloat16)
        return jnp.einsum("hna,ahd->nhd", probs, values_part, preferred_element_type=jnp.float32)

    outputs = lax.map(query_block, jnp.arange(blocks, dtype=jnp.int32))
    attended = outputs.transpose(1, 0, 2, 3).reshape(FRAMES, ROWS_DEV, COLUMNS, D)
    local_mix = mix_local(window, conv_weight)
    mixed = (attended + local_mix).astype(jnp.bfloat16)
    return mixed.reshape(value_states.shape)


def mesh_copy(src, dst, send, recv, device):
    return pltpu.make_async_remote_copy(
        src_ref=src,
        dst_ref=dst,
        send_sem=send,
        recv_sem=recv,
        device_id=device,
        device_id_type=MESH,
    )


def fused(
    n_tm,
    n_sp,
    q_ref,
    k_ref,
    v_ref,
    w_ref,
    out_ref,
    pool_s,
    gather,
    agents_s,
    blocks_s,
    parts_out,
    parts_in,
    stats,
    av_in,
    avt_s,
    wt_s,
    rows,
    acc_s,
    prev_out,
    next_out,
    prev_in,
    next_in,
    res_out,
    res_in,
    ag_sem,
    st_sem,
    pt_sem,
    av_sem,
    pair_sem,
    side_send,
    side_recv,
    time_send,
    time_recv,
    res_sem,
):
    f32, bf16 = jnp.float32, jnp.bfloat16
    tm, me = lax.axis_index("tm"), lax.axis_index("space")
    par = lax.rem(me, 2)
    z = me // 2
    partner = me + 1 - 2 * par
    has_lo, has_hi = z > 0, z < n_sp // 2 - 1
    has_prev, has_next = tm > 0, tm < n_tm - 1
    inv_root = HEAD_DIM ** (-0.5)
    frames, cols, width = v_ref.shape
    tokens = frames * cols
    half = width // 2
    n_chunk, lc = rows.shape[0], rows.shape[4]
    n_block = n_chunk * 2
    agents = AGENT_DEV * n_sp
    per = lc // HEAD_DIM
    ha = per * agents
    piece = gather.shape[2]
    n_piece = width // piece
    lanes_half = n_chunk * ha
    nt = (((1,), (1,)), ((), ()))

    barrier = pltpu.get_barrier_semaphore()
    peers = [lax.rem(me + d, n_sp) for d in range(n_sp)]
    sources = [lax.rem(me + n_sp - d, n_sp) for d in range(n_sp)]
    for d in range(1, n_sp):
        pl.semaphore_signal(barrier, inc=1, device_id=(tm, peers[d]), device_id_type=MESH)

    @pl.when(has_prev)
    def _():
        pl.semaphore_signal(barrier, inc=1, device_id=(tm - 1, me), device_id_type=MESH)

    @pl.when(has_next)
    def _():
        pl.semaphore_signal(barrier, inc=1, device_id=(tm + 1, me), device_id_type=MESH)

    summed = q_ref[0].astype(f32)
    for f in range(1, frames):
        summed = summed + q_ref[f].astype(f32)
    group = cols // AGENT_DEV
    for j in range(AGENT_DEV):
        mean = jnp.sum(summed[j * group : (j + 1) * group], axis=0, keepdims=True) * (
            1.0 / (frames * group)
        )
        for p in range(n_piece):
            pool_s[p * AGENT_DEV + j : p * AGENT_DEV + j + 1, :] = mean[:, p * piece : (p + 1) * piece]
    gather[me] = pool_s[...].astype(bf16)

    greeted = n_sp - 1 + jnp.where(has_prev, 1, 0) + jnp.where(has_next, 1, 0)
    pl.semaphore_wait(barrier, greeted)

    def to_all(src_of, dst, sem):
        return [
            mesh_copy(src_of(d), dst.at[me], sem.at[0, d], sem.at[1, d], (tm, peers[d]))
            for d in range(1, n_sp)
        ]

    def from_all(dst, sem):
        for d in range(1, n_sp):
            mesh_copy(
                dst.at[sources[d]], dst.at[sources[d]], sem.at[0, d], sem.at[1, d], (tm, peers[d])
            ).wait_recv()

    ag = to_all(lambda d: gather.at[me], gather, ag_sem)
    for copy in ag:
        copy.start()

    def lanes_of(side, c):
        return pl.ds(pl.multiple_of(side * half + c * lc, lc), lc)

    pair = []
    for c in range(n_chunk):
        copy = mesh_copy(
            v_ref.at[:, :, lanes_of(1 - par, c)],
            rows.at[c, 1 + par],
            pair_sem.at[0, c],
            pair_sem.at[1, c],
            (tm, partner),
        )
        copy.start()
        pair.append(copy)

    direct_ok = jnp.where(par == 0, z, n_sp // 2 - 1 - z) > 0
    forward_ok = jnp.where(par == 0, n_sp // 2 - 1 - z, z) > 0
    direct_to = me + 4 * par - 2
    forward_to = me + 2 - 4 * par
    direct = [
        mesh_copy(
            v_ref.at[:, :, lanes_of(par, c)],
            rows.at[c, 3 - 3 * par],
            side_send.at[0, c],
            side_recv.at[1 - par, c],
            (tm, direct_to),
        )
        for c in range(n_chunk)
    ]
    forward = [
        mesh_copy(
            rows.at[c, 2 - par],
            rows.at[c, 3 * par],
            side_send.at[1, c],
            side_recv.at[par, c],
            (tm, forward_to),
        )
        for c in range(n_chunk)
    ]

    @pl.when(direct_ok)
    def _():
        for c in range(n_chunk):
            direct[c].start()

    def pass_on(c):
        mesh_copy(
            v_ref.at[:, :, lanes_of(1 - par, c)],
            rows.at[c, 2 - par],
            pair_sem.at[0, c],
            pair_sem.at[1, c],
            (tm, partner),
        ).wait_recv()

        @pl.when(forward_ok)
        def _():
            forward[c].start()

    zero_row = jnp.zeros((frames, cols, lc), bf16)
    zero_part = jnp.zeros(prev_in.shape, bf16)
    for c in range(n_chunk):
        rows[c, 1 + par] = v_ref[:, :, lanes_of(par, c)]

        @pl.when(z == 0)
        def _():
            rows[c, 0] = zero_row

        @pl.when(z == n_sp // 2 - 1)
        def _():
            rows[c, 3] = zero_row

    @pl.when(tm == 0)
    def _():
        prev_in[...] = zero_part

    @pl.when(tm == n_tm - 1)
    def _():
        next_in[...] = zero_part

    pass_on(0)
    from_all(gather, ag_sem)

    packed = gather[...].reshape(n_sp * n_piece * AGENT_DEV, piece)
    row = lax.broadcasted_iota(jnp.int32, (agents, packed.shape[0]), 0)
    col = lax.broadcasted_iota(jnp.int32, (agents, packed.shape[0]), 1)
    span = n_piece * AGENT_DEV
    for p in range(n_piece):
        wanted = (row // AGENT_DEV) * span + p * AGENT_DEV + lax.rem(row, AGENT_DEV)
        pick = jnp.where(col == wanted, 1.0, 0.0).astype(bf16)
        agents_s[:, p * piece : (p + 1) * piece] = jnp.dot(
            pick, packed, preferred_element_type=f32
        ).astype(bf16)

    ch = lax.broadcasted_iota(jnp.int32, (agents, lc), 1) // HEAD_DIM
    lane_head = lax.broadcasted_iota(jnp.int32, (HEAD_DIM, ha), 1) // agents
    for b in range(n_block):
        block = agents_s[:, b * lc : (b + 1) * lc].astype(f32)
        blocks_s[b] = jnp.concatenate(
            [jnp.where(ch == h, block, 0.0) for h in range(per)], axis=0
        ).astype(bf16)

    compact = []
    for b in range(n_block):
        keys = k_ref[:, b * lc : (b + 1) * lc]
        scores = lax.dot_general(keys, blocks_s[b], nt, preferred_element_type=f32) * inv_root
        peak = jnp.max(scores, axis=0, keepdims=True)
        weights = jnp.exp(scores - peak)
        at = slice(b * ha, (b + 1) * ha)
        stats[me, 0:1, at] = peak
        stats[me, 1:2, at] = jnp.sum(weights, axis=0, keepdims=True)
        values = v_ref[:, :, b * lc : (b + 1) * lc].reshape(tokens, lc)
        full = lax.dot_general(
            values, weights.astype(bf16), (((0,), (0,)), ((), ())), preferred_element_type=f32
        )
        small = jnp.where(lane_head == 0, full[0:HEAD_DIM], 0.0)
        for h in range(1, per):
            small = jnp.where(lane_head == h, full[h * HEAD_DIM : (h + 1) * HEAD_DIM], small)
        compact.append(small)
    st = to_all(lambda d: stats.at[me], stats, st_sem)
    for copy in st:
        copy.start()
    low = jnp.concatenate(compact[:n_chunk], axis=1)
    high = jnp.concatenate(compact[n_chunk:], axis=1)
    each = HEAD_DIM // n_sp
    for s in range(n_sp):
        at = slice(s * each, (s + 1) * each)
        parts_out[s] = jnp.concatenate([low[at], high[at]], axis=0).astype(bf16)
    pt = to_all(lambda d: parts_out.at[peers[d]], parts_in, pt_sem)
    for copy in pt:
        copy.start()
    parts_in[me] = parts_out[me]

    for c in range(1, n_chunk):
        pass_on(c)

    for b in range(n_block):
        asked = q_ref[:, :, b * lc : (b + 1) * lc].reshape(tokens, lc)
        scores = lax.dot_general(blocks_s[b], asked, nt, preferred_element_type=f32) * inv_root
        scores = scores.reshape(per, agents, tokens)
        raised = jnp.exp(scores - jnp.max(scores, axis=1, keepdims=True))
        probs = raised / jnp.sum(raised, axis=1, keepdims=True)
        wt_s[b] = probs.reshape(ha, tokens).T.astype(bf16)

    column = lax.broadcasted_iota(jnp.int32, (cols, 128), 0)

    def convolve(c):
        @pl.when(has_lo)
        def _():
            mesh_copy(
                rows.at[c, 0], rows.at[c, 0], side_send.at[0, c], side_recv.at[0, c], (tm, partner)
            ).wait_recv()

        @pl.when(has_hi)
        def _():
            mesh_copy(
                rows.at[c, 3], rows.at[c, 3], side_send.at[0, c], side_recv.at[1, c], (tm, partner)
            ).wait_recv()

        def tile(step, carry):
            o, sub = step // (lc // 128), lax.rem(step, lc // 128)
            at = pl.ds(pl.multiple_of(sub * 128, 128), 128)
            w_at = pl.ds(pl.multiple_of(par * half + c * lc + sub * 128, 128), 128)
            for out_f in range(-1, frames + 1):
                sums = [None, None, None]
                for i in range(3):
                    f = out_f + i - 1
                    if f < 0 or f >= frames:
                        continue
                    for j in range(3):
                        x = rows[c, o + j, f, :, at].astype(f32)
                        for k in range(3):
                            tap = i * 9 + j * 3 + k
                            term = x * w_ref[tap : tap + 1, w_at]
                            sums[k] = term if sums[k] is None else sums[k] + term
                before = jnp.where(column == 0, 0.0, pltpu.roll(sums[0], 1, 0))
                after = jnp.where(column == cols - 1, 0.0, pltpu.roll(sums[2], cols - 1, 0))
                total = sums[1] + before + after
                if out_f < 0:
                    prev_out[c, o, :, at] = total.astype(bf16)
                elif out_f == frames:
                    next_out[c, o, :, at] = total.astype(bf16)
                else:
                    acc_s[c, o, out_f, :, at] = total
            return carry

        lax.fori_loop(0, 2 * (lc // 128), tile, 0)

        @pl.when(has_prev)
        def _():
            to_prev[c].start()

        @pl.when(has_next)
        def _():
            to_next[c].start()

    to_prev = [
        mesh_copy(
            prev_out.at[c], next_in.at[c], time_send.at[0, c], time_recv.at[0, c], (tm - 1, me)
        )
        for c in range(n_chunk)
    ]
    to_next = [
        mesh_copy(
            next_out.at[c], prev_in.at[c], time_send.at[1, c], time_recv.at[1, c], (tm + 1, me)
        )
        for c in range(n_chunk)
    ]
    result = [
        mesh_copy(res_out.at[c], res_in.at[c], res_sem.at[0, c], res_sem.at[1, c], (tm, partner))
        for c in range(n_chunk)
    ]

    def finish(c):
        @pl.when(has_prev)
        def _():
            to_next[c].wait_recv()

        @pl.when(has_next)
        def _():
            to_prev[c].wait_recv()

        for o in range(2):
            acc_s[c, o, 0] += prev_in[c, o].astype(f32)
            acc_s[c, o, frames - 1] += next_in[c, o].astype(f32)
        res_out[c] = acc_s[c, 1 - par].astype(bf16)
        result[c].start()

    convolve(0)

    from_all(stats, st_sem)
    from_all(parts_in, pt_sem)
    peaks = stats[:, 0:1, :]
    totals = stats[:, 1:2, :]
    top = jnp.max(peaks, axis=0)
    total = jnp.zeros_like(top)
    merged = [jnp.zeros((each, lanes_half), f32) for _ in range(2)]
    for s in range(n_sp):
        scale = jnp.exp(peaks[s] - top)
        total = total + scale * totals[s]
        part = parts_in[s].astype(f32)
        for g in range(2):
            merged[g] = merged[g] + part[g * each : (g + 1) * each] * scale[
                :, g * lanes_half : (g + 1) * lanes_half
            ]
    av_in[me] = jnp.concatenate(
        [merged[g] / total[:, g * lanes_half : (g + 1) * lanes_half] for g in range(2)], axis=0
    ).astype(bf16)
    av = to_all(lambda d: av_in.at[me], av_in, av_sem)
    for copy in av:
        copy.start()

    for c in range(1, n_chunk):
        convolve(c)
        finish(c - 1)
    finish(n_chunk - 1)

    from_all(av_in, av_sem)
    spread = av_in[...].astype(f32)
    for g in range(2):
        avt_s[g] = (
            spread[:, g * each : (g + 1) * each, :].reshape(HEAD_DIM, lanes_half).astype(bf16)
        )

    def attended(side, c):
        small = avt_s[side, :, c * ha : (c + 1) * ha].astype(f32)
        spread_values = jnp.concatenate(
            [jnp.where(lane_head == h, small, 0.0) for h in range(per)], axis=0
        ).astype(bf16)
        got = lax.dot_general(
            wt_s[side * n_chunk + c], spread_values, nt, preferred_element_type=f32
        )
        return got.reshape(frames, cols, lc)

    for c in range(n_chunk):
        out_ref[:, :, lanes_of(par, c)] = (attended(par, c) + acc_s[c, par]).astype(bf16)
    for c in range(n_chunk):
        result[c].wait_recv()
        out_ref[:, :, lanes_of(1 - par, c)] = (
            attended(1 - par, c) + res_in[c].astype(f32)
        ).astype(bf16)

    for copy in ag + st + pt + av + pair + result:
        copy.wait_send()

    @pl.when(direct_ok)
    def _():
        for c in range(n_chunk):
            direct[c].wait_send()

    @pl.when(forward_ok)
    def _():
        for c in range(n_chunk):
            forward[c].wait_send()

    @pl.when(has_prev)
    def _():
        for c in range(n_chunk):
            to_prev[c].wait_send()

    @pl.when(has_next)
    def _():
        for c in range(n_chunk):
            to_next[c].wait_send()


def on_device_fused(queries, key_states, value_states, conv_weight):
    n_tm, n_sp = lax.axis_size("tm"), lax.axis_size("space")
    tokens = FRAMES * ROWS_DEV * COLUMNS
    lc = 4 * HEAD_DIM
    n_chunk = D // 2 // lc
    agents = AGENT_DEV * n_sp
    ha = lc // HEAD_DIM * agents
    each = HEAD_DIM // n_sp
    n_piece = 16 // AGENT_DEV
    piece = D // n_piece
    f32, bf16 = jnp.float32, jnp.bfloat16
    dma = pltpu.SemaphoreType.DMA
    side = (n_chunk, 2, COLUMNS, lc)
    whole = (n_chunk, FRAMES, COLUMNS, lc)
    vmem = pl.BlockSpec(memory_space=pltpu.VMEM)
    mixed = pl.pallas_call(
        functools.partial(fused, n_tm, n_sp),
        out_shape=jax.ShapeDtypeStruct((FRAMES, COLUMNS, D), bf16),
        in_specs=[vmem] * 4,
        out_specs=vmem,
        scratch_shapes=[
            pltpu.VMEM((16, piece), f32),
            pltpu.VMEM((n_sp, 16, piece), bf16),
            pltpu.VMEM((agents, D), bf16),
            pltpu.VMEM((2 * n_chunk, ha, lc), bf16),
            pltpu.VMEM((n_sp, 2 * each, n_chunk * ha), bf16),
            pltpu.VMEM((n_sp, 2 * each, n_chunk * ha), bf16),
            pltpu.VMEM((n_sp, 2, 2 * n_chunk * ha), f32),
            pltpu.VMEM((n_sp, 2 * each, n_chunk * ha), bf16),
            pltpu.VMEM((2, HEAD_DIM, n_chunk * ha), bf16),
            pltpu.VMEM((2 * n_chunk, tokens, ha), bf16),
            pltpu.VMEM((n_chunk, 4, FRAMES, COLUMNS, lc), bf16),
            pltpu.VMEM((n_chunk, 2, FRAMES, COLUMNS, lc), f32),
            pltpu.VMEM(side, bf16),
            pltpu.VMEM(side, bf16),
            pltpu.VMEM(side, bf16),
            pltpu.VMEM(side, bf16),
            pltpu.VMEM(whole, bf16),
            pltpu.VMEM(whole, bf16),
            dma((2, n_sp)),
            dma((2, n_sp)),
            dma((2, n_sp)),
            dma((2, n_sp)),
            dma((2, n_chunk)),
            dma((2, n_chunk)),
            dma((2, n_chunk)),
            dma((2, n_chunk)),
            dma((2, n_chunk)),
            dma((2, n_chunk)),
        ],
        compiler_params=pltpu.CompilerParams(
            collective_id=0, has_side_effects=True, vmem_limit_bytes=48 * 1024 * 1024
        ),
    )(
        queries.reshape(FRAMES, COLUMNS, D),
        key_states.reshape(tokens, D),
        value_states.reshape(FRAMES, COLUMNS, D),
        conv_weight.reshape(27, D),
    )
    return mixed.reshape(value_states.shape)


def solution(mesh):
    fits = mesh.shape["space"] * 8 == HEAD_DIM
    return jax.shard_map(
        on_device_fused if fits else on_device,
        mesh=mesh,
        in_specs=(
            P("tm", None, "space", None, None),
            P("tm", None, "space", None, None),
            P("tm", None, "space", None, None),
            P(),
        ),
        out_specs=P("tm", None, "space", None, None),
        check_vma=False,
    )
```

```python
import functools
import math

import jax
import jax.numpy as jnp
from jax import lax
from jax.experimental import pallas as pl
from jax.experimental.pallas import tpu as pltpu
from jax.sharding import PartitionSpec as P

HEADS = 24
HEAD_DIM = 64
D = 1536
FRAMES = 4
ROWS_DEV = 1
COLUMNS = 32
AGENT_DEV = 4
MESH = pl.DeviceIdType.MESH


def extended(cells, sides, width):
    for axis, dim in sides:
        count = lax.axis_size(axis)
        ends = count - 1
        head = lax.slice_in_dim(cells, 0, width, axis=dim)
        tail = lax.slice_in_dim(cells, cells.shape[dim] - width, cells.shape[dim], axis=dim)
        cells = jnp.concatenate(
            [
                lax.ppermute(tail, axis, [(i, (i + 1) % count) for i in range(ends)]),
                cells,
                lax.ppermute(head, axis, [((i + 1) % count, i) for i in range(ends)]),
            ],
            axis=dim,
        )
    return cells


def merged_2(part, axis, combine):
    gathered = jax.tree.map(lambda a: lax.all_gather(a, axis), part)

    def take(source):
        return jax.tree.map(lambda a: lax.dynamic_index_in_dim(a, source, 0, False), gathered)

    return lax.fori_loop(
        1, lax.axis_size(axis), lambda source, state: combine(state, take(source)), take(0)
    )


def mix_local(window, conv_weight):
    shape = (window.shape[0] - 2, window.shape[1] - 2, window.shape[2] - 2, window.shape[3])
    total = jnp.zeros(shape, jnp.float32)
    for time_off in range(3):
        for row_off in range(3):
            for col_off in range(3):
                piece = window[
                    time_off : time_off + shape[0],
                    row_off : row_off + shape[1],
                    col_off : col_off + shape[2],
                ]
                total = total + piece.astype(jnp.float32) * conv_weight[time_off, row_off, col_off]
    return total


def pair_merge(first, second):
    peak = jnp.maximum(first[0], second[0])
    left = jnp.exp(first[0] - peak)
    right = jnp.exp(second[0] - peak)
    return (
        peak,
        first[1] * left + second[1] * right,
        first[2] * left[..., None] + second[2] * right[..., None],
    )


def on_device(queries, key_states, value_states, conv_weight):
    tokens = FRAMES * ROWS_DEV * COLUMNS
    inv_root = HEAD_DIM ** (-0.5)
    per_block = math.gcd(HEADS, 8)
    blocks = HEADS // per_block
    padded = extended(value_states, (("tm", 1), ("space", 2)), 1)
    window = jnp.pad(padded[0], ((0, 0), (0, 0), (1, 1), (0, 0)))
    pooled = jnp.mean(
        queries.reshape(FRAMES, ROWS_DEV, AGENT_DEV, COLUMNS // AGENT_DEV, D),
        axis=(0, 1, 3),
        dtype=jnp.float32,
    )
    agents = lax.all_gather(pooled.astype(jnp.bfloat16), "space", axis=0, tiled=True)
    count = agents.shape[0]
    agent_heads = agents.reshape(count, HEADS, HEAD_DIM)
    query_heads = queries.reshape(tokens, HEADS, HEAD_DIM)
    key_heads = key_states.reshape(tokens, HEADS, HEAD_DIM)
    value_heads = value_states.reshape(tokens, HEADS, HEAD_DIM)

    def agent_block(index):
        start = index * per_block
        agent_part = lax.dynamic_slice_in_dim(agent_heads, start, per_block, 1)
        key_part = lax.dynamic_slice_in_dim(key_heads, start, per_block, 1)
        value_part = lax.dynamic_slice_in_dim(value_heads, start, per_block, 1)
        scores = (
            jnp.einsum("ahd,nhd->ahn", agent_part, key_part, preferred_element_type=jnp.float32)
            * inv_root
        )
        block_peak = jnp.max(scores, axis=2)
        weights = jnp.exp(scores - block_peak[..., None])
        block_total = jnp.sum(weights, axis=2)
        block_acc = jnp.einsum(
            "ahn,nhd->ahd",
            weights.astype(jnp.bfloat16),
            value_part,
            preferred_element_type=jnp.float32,
        )
        return (block_peak, block_total, block_acc)

    peaks, totals, accs = lax.map(agent_block, jnp.arange(blocks, dtype=jnp.int32))
    local_peak = peaks.transpose(1, 0, 2).reshape(count, HEADS)
    local_total = totals.transpose(1, 0, 2).reshape(count, HEADS)
    local_acc = accs.transpose(1, 0, 2, 3).reshape(count, HEADS, HEAD_DIM)
    merged = merged_2((local_peak, local_total, local_acc), "space", pair_merge)
    agent_values = (merged[2] / merged[1][..., None]).astype(jnp.bfloat16)

    def query_block(index):
        start = index * per_block
        query_part = lax.dynamic_slice_in_dim(query_heads, start, per_block, 1)
        agent_part = lax.dynamic_slice_in_dim(agent_heads, start, per_block, 1)
        values_part = lax.dynamic_slice_in_dim(agent_values, start, per_block, 1)
        query_scores = (
            jnp.einsum("nhd,ahd->hna", query_part, agent_part, preferred_element_type=jnp.float32)
            * inv_root
        )
        probs = jax.nn.softmax(query_scores, axis=-1).astype(jnp.bfloat16)
        return jnp.einsum("hna,ahd->nhd", probs, values_part, preferred_element_type=jnp.float32)

    outputs = lax.map(query_block, jnp.arange(blocks, dtype=jnp.int32))
    attended = outputs.transpose(1, 0, 2, 3).reshape(FRAMES, ROWS_DEV, COLUMNS, D)
    local_mix = mix_local(window, conv_weight)
    mixed = (attended + local_mix).astype(jnp.bfloat16)
    return mixed.reshape(value_states.shape)


def mesh_copy(src, dst, send, recv, device):
    return pltpu.make_async_remote_copy(
        src_ref=src,
        dst_ref=dst,
        send_sem=send,
        recv_sem=recv,
        device_id=device,
        device_id_type=MESH,
    )


def fused(
    n_tm,
    n_sp,
    q_hbm,
    k_hbm,
    v_hbm,
    w_hbm,
    out_ref,
    q_ref,
    k_ref,
    v_ref,
    w_ref,
    pool_s,
    gather,
    agents_s,
    blocks_s,
    parts_out,
    parts_in,
    stats,
    av_in,
    avt_s,
    wt_s,
    rows,
    acc_s,
    prev_out,
    next_out,
    prev_in,
    next_in,
    res_out,
    res_in,
    ag_sem,
    st_sem,
    pt_sem,
    av_sem,
    pair_sem,
    side_send,
    side_recv,
    time_send,
    time_recv,
    res_sem,
    in_sem,
):
    loads = [
        pltpu.make_async_copy(source, held, in_sem.at[i])
        for i, (source, held) in enumerate(
            ((q_hbm, q_ref), (v_hbm, v_ref), (k_hbm, k_ref), (w_hbm, w_ref))
        )
    ]
    for load in loads:
        load.start()
    q_load, v_load, k_load, w_load = loads
    f32, bf16 = jnp.float32, jnp.bfloat16
    tm, me = lax.axis_index("tm"), lax.axis_index("space")
    par = lax.rem(me, 2)
    z = me // 2
    partner = me + 1 - 2 * par
    has_lo, has_hi = z > 0, z < n_sp // 2 - 1
    has_prev, has_next = tm > 0, tm < n_tm - 1
    inv_root = HEAD_DIM ** (-0.5)
    frames, cols, width = v_ref.shape
    tokens = frames * cols
    half = width // 2
    n_chunk, lc = rows.shape[0], rows.shape[4]
    n_block = n_chunk * 2
    agents = AGENT_DEV * n_sp
    per = lc // HEAD_DIM
    ha = per * agents
    piece = gather.shape[2]
    n_piece = width // piece
    lanes_half = n_chunk * ha
    nt = (((1,), (1,)), ((), ()))

    barrier = pltpu.get_barrier_semaphore()
    peers = [lax.rem(me + d, n_sp) for d in range(n_sp)]
    sources = [lax.rem(me + n_sp - d, n_sp) for d in range(n_sp)]
    for d in range(1, n_sp):
        pl.semaphore_signal(barrier, inc=1, device_id=(tm, peers[d]), device_id_type=MESH)

    @pl.when(has_prev)
    def _():
        pl.semaphore_signal(barrier, inc=1, device_id=(tm - 1, me), device_id_type=MESH)

    @pl.when(has_next)
    def _():
        pl.semaphore_signal(barrier, inc=1, device_id=(tm + 1, me), device_id_type=MESH)

    q_load.wait()
    summed = q_ref[0].astype(f32)
    for f in range(1, frames):
        summed = summed + q_ref[f].astype(f32)
    group = cols // AGENT_DEV
    for j in range(AGENT_DEV):
        mean = jnp.sum(summed[j * group : (j + 1) * group], axis=0, keepdims=True) * (
            1.0 / (frames * group)
        )
        for p in range(n_piece):
            pool_s[p * AGENT_DEV + j : p * AGENT_DEV + j + 1, :] = mean[:, p * piece : (p + 1) * piece]
    gather[me] = pool_s[...].astype(bf16)

    greeted = n_sp - 1 + jnp.where(has_prev, 1, 0) + jnp.where(has_next, 1, 0)
    pl.semaphore_wait(barrier, greeted)

    def to_all(src_of, dst, sem):
        return [
            mesh_copy(src_of(d), dst.at[me], sem.at[0, d], sem.at[1, d], (tm, peers[d]))
            for d in range(1, n_sp)
        ]

    def from_all(dst, sem):
        for d in range(1, n_sp):
            mesh_copy(
                dst.at[sources[d]], dst.at[sources[d]], sem.at[0, d], sem.at[1, d], (tm, peers[d])
            ).wait_recv()

    ag = to_all(lambda d: gather.at[me], gather, ag_sem)
    for copy in ag:
        copy.start()

    v_load.wait()

    def lanes_of(side, c):
        return pl.ds(pl.multiple_of(side * half + c * lc, lc), lc)

    pair = []
    for c in range(n_chunk):
        copy = mesh_copy(
            v_ref.at[:, :, lanes_of(1 - par, c)],
            rows.at[c, 1 + par],
            pair_sem.at[0, c],
            pair_sem.at[1, c],
            (tm, partner),
        )
        copy.start()
        pair.append(copy)

    direct_ok = jnp.where(par == 0, z, n_sp // 2 - 1 - z) > 0
    forward_ok = jnp.where(par == 0, n_sp // 2 - 1 - z, z) > 0
    direct_to = me + 4 * par - 2
    forward_to = me + 2 - 4 * par
    direct = [
        mesh_copy(
            v_ref.at[:, :, lanes_of(par, c)],
            rows.at[c, 3 - 3 * par],
            side_send.at[0, c],
            side_recv.at[1 - par, c],
            (tm, direct_to),
        )
        for c in range(n_chunk)
    ]
    forward = [
        mesh_copy(
            rows.at[c, 2 - par],
            rows.at[c, 3 * par],
            side_send.at[1, c],
            side_recv.at[par, c],
            (tm, forward_to),
        )
        for c in range(n_chunk)
    ]

    @pl.when(direct_ok)
    def _():
        for c in range(n_chunk):
            direct[c].start()

    def pass_on(c):
        mesh_copy(
            v_ref.at[:, :, lanes_of(1 - par, c)],
            rows.at[c, 2 - par],
            pair_sem.at[0, c],
            pair_sem.at[1, c],
            (tm, partner),
        ).wait_recv()

        @pl.when(forward_ok)
        def _():
            forward[c].start()

    zero_row = jnp.zeros((frames, cols, lc), bf16)
    zero_part = jnp.zeros(prev_in.shape, bf16)
    for c in range(n_chunk):
        rows[c, 1 + par] = v_ref[:, :, lanes_of(par, c)]

        @pl.when(z == 0)
        def _():
            rows[c, 0] = zero_row

        @pl.when(z == n_sp // 2 - 1)
        def _():
            rows[c, 3] = zero_row

    @pl.when(tm == 0)
    def _():
        prev_in[...] = zero_part

    @pl.when(tm == n_tm - 1)
    def _():
        next_in[...] = zero_part

    pass_on(0)
    from_all(gather, ag_sem)

    packed = gather[...].reshape(n_sp * n_piece * AGENT_DEV, piece)
    row = lax.broadcasted_iota(jnp.int32, (agents, packed.shape[0]), 0)
    col = lax.broadcasted_iota(jnp.int32, (agents, packed.shape[0]), 1)
    span = n_piece * AGENT_DEV
    for p in range(n_piece):
        wanted = (row // AGENT_DEV) * span + p * AGENT_DEV + lax.rem(row, AGENT_DEV)
        pick = jnp.where(col == wanted, 1.0, 0.0).astype(bf16)
        agents_s[:, p * piece : (p + 1) * piece] = jnp.dot(
            pick, packed, preferred_element_type=f32
        ).astype(bf16)

    ch = lax.broadcasted_iota(jnp.int32, (agents, lc), 1) // HEAD_DIM
    lane_head = lax.broadcasted_iota(jnp.int32, (HEAD_DIM, ha), 1) // agents
    for b in range(n_block):
        block = agents_s[:, b * lc : (b + 1) * lc].astype(f32)
        blocks_s[b] = jnp.concatenate(
            [jnp.where(ch == h, block, 0.0) for h in range(per)], axis=0
        ).astype(bf16)

    k_load.wait()
    compact = []
    for b in range(n_block):
        if 0 < b < n_chunk:
            pass_on(b)
        keys = k_ref[:, b * lc : (b + 1) * lc]
        scores = lax.dot_general(keys, blocks_s[b], nt, preferred_element_type=f32) * inv_root
        peak = jnp.max(scores, axis=0, keepdims=True)
        weights = jnp.exp(scores - peak)
        at = slice(b * ha, (b + 1) * ha)
        sums = jnp.sum(weights, axis=0, keepdims=True)
        stats[me, 0:1, at] = peak + jnp.log(sums)
        values = v_ref[:, :, b * lc : (b + 1) * lc].reshape(tokens, lc)
        full = lax.dot_general(
            values, weights.astype(bf16), (((0,), (0,)), ((), ())), preferred_element_type=f32
        )
        small = jnp.where(lane_head == 0, full[0:HEAD_DIM], 0.0)
        for h in range(1, per):
            small = jnp.where(lane_head == h, full[h * HEAD_DIM : (h + 1) * HEAD_DIM], small)
        compact.append(small / sums)
    st = to_all(lambda d: stats.at[me], stats, st_sem)
    for copy in st:
        copy.start()
    low = jnp.concatenate(compact[:n_chunk], axis=1)
    high = jnp.concatenate(compact[n_chunk:], axis=1)
    each = HEAD_DIM // n_sp
    for s in range(n_sp):
        at = slice(s * each, (s + 1) * each)
        parts_out[s] = jnp.concatenate([low[at], high[at]], axis=0).astype(bf16)
    pt = to_all(lambda d: parts_out.at[peers[d]], parts_in, pt_sem)
    for copy in pt:
        copy.start()
    parts_in[me] = parts_out[me]

    for b in range(n_block):
        asked = q_ref[:, :, b * lc : (b + 1) * lc].reshape(tokens, lc)
        scores = lax.dot_general(blocks_s[b], asked, nt, preferred_element_type=f32) * inv_root
        scores = scores.reshape(per, agents, tokens)
        raised = jnp.exp(scores - jnp.max(scores, axis=1, keepdims=True))
        probs = raised / jnp.sum(raised, axis=1, keepdims=True)
        wt_s[b] = probs.reshape(ha, tokens).T.astype(bf16)

    column = lax.broadcasted_iota(jnp.int32, (cols, 128), 0)

    def convolve(c):
        @pl.when(has_lo)
        def _():
            mesh_copy(
                rows.at[c, 0], rows.at[c, 0], side_send.at[0, c], side_recv.at[0, c], (tm, partner)
            ).wait_recv()

        @pl.when(has_hi)
        def _():
            mesh_copy(
                rows.at[c, 3], rows.at[c, 3], side_send.at[0, c], side_recv.at[1, c], (tm, partner)
            ).wait_recv()

        def tile(step, carry):
            o, sub = step // (lc // 128), lax.rem(step, lc // 128)
            at = pl.ds(pl.multiple_of(sub * 128, 128), 128)
            w_at = pl.ds(pl.multiple_of(par * half + c * lc + sub * 128, 128), 128)
            for out_f in range(-1, frames + 1):
                sums = [None, None, None]
                for i in range(3):
                    f = out_f + i - 1
                    if f < 0 or f >= frames:
                        continue
                    for j in range(3):
                        x = rows[c, o + j, f, :, at].astype(f32)
                        for k in range(3):
                            term = x * w_ref[i, j, k : k + 1, w_at]
                            sums[k] = term if sums[k] is None else sums[k] + term
                before = jnp.where(column == 0, 0.0, pltpu.roll(sums[0], 1, 0))
                after = jnp.where(column == cols - 1, 0.0, pltpu.roll(sums[2], cols - 1, 0))
                total = sums[1] + before + after
                if out_f < 0:
                    prev_out[c, o, :, at] = total.astype(bf16)
                elif out_f == frames:
                    next_out[c, o, :, at] = total.astype(bf16)
                else:
                    acc_s[c, o, out_f, :, at] = total
            return carry

        lax.fori_loop(0, 2 * (lc // 128), tile, 0)

        @pl.when(has_prev)
        def _():
            to_prev[c].start()

        @pl.when(has_next)
        def _():
            to_next[c].start()

        res_out[c, 1:last] = acc_s[c, 1 - par, 1:last].astype(bf16)
        inner[c].start()

    to_prev = [
        mesh_copy(
            prev_out.at[c], next_in.at[c], time_send.at[0, c], time_recv.at[0, c], (tm - 1, me)
        )
        for c in range(n_chunk)
    ]
    to_next = [
        mesh_copy(
            next_out.at[c], prev_in.at[c], time_send.at[1, c], time_recv.at[1, c], (tm + 1, me)
        )
        for c in range(n_chunk)
    ]
    last = frames - 1
    inner = [
        mesh_copy(
            res_out.at[c, 1:last],
            res_in.at[c, 1:last],
            res_sem.at[0, c],
            res_sem.at[1, c],
            (tm, partner),
        )
        for c in range(n_chunk)
    ]
    outer = [
        mesh_copy(
            res_out.at[c, f],
            res_in.at[c, f],
            res_sem.at[0, (e + 1) * n_chunk + c],
            res_sem.at[1, (e + 1) * n_chunk + c],
            (tm, partner),
        )
        for c in range(n_chunk)
        for e, f in enumerate((0, last))
    ]

    def finish(c):
        @pl.when(has_prev)
        def _():
            to_next[c].wait_recv()

        @pl.when(has_next)
        def _():
            to_prev[c].wait_recv()

        for o in range(2):
            acc_s[c, o, 0] += prev_in[c, o].astype(f32)
            acc_s[c, o, frames - 1] += next_in[c, o].astype(f32)
        for e, f in enumerate((0, last)):
            res_out[c, f] = acc_s[c, 1 - par, f].astype(bf16)
            outer[2 * c + e].start()

    w_load.wait()
    convolve(0)

    from_all(stats, st_sem)
    from_all(parts_in, pt_sem)
    peaks = stats[...]
    top = jnp.max(peaks, axis=0)
    total = jnp.zeros_like(top)
    merged = [jnp.zeros((each, lanes_half), f32) for _ in range(2)]
    for s in range(n_sp):
        scale = jnp.exp(peaks[s] - top)
        total = total + scale
        part = parts_in[s].astype(f32)
        for g in range(2):
            merged[g] = merged[g] + part[g * each : (g + 1) * each] * scale[
                :, g * lanes_half : (g + 1) * lanes_half
            ]
    av_in[me] = jnp.concatenate(
        [merged[g] / total[:, g * lanes_half : (g + 1) * lanes_half] for g in range(2)], axis=0
    ).astype(bf16)
    av = to_all(lambda d: av_in.at[me], av_in, av_sem)
    for copy in av:
        copy.start()

    for c in range(1, n_chunk):
        convolve(c)
        finish(c - 1)
    finish(n_chunk - 1)

    from_all(av_in, av_sem)
    spread = av_in[...].astype(f32)
    for g in range(2):
        avt_s[g] = (
            spread[:, g * each : (g + 1) * each, :].reshape(HEAD_DIM, lanes_half).astype(bf16)
        )

    def attended(side, c):
        small = avt_s[side, :, c * ha : (c + 1) * ha].astype(f32)
        spread_values = jnp.concatenate(
            [jnp.where(lane_head == h, small, 0.0) for h in range(per)], axis=0
        ).astype(bf16)
        got = lax.dot_general(
            wt_s[side * n_chunk + c], spread_values, nt, preferred_element_type=f32
        )
        return got.reshape(frames, cols, lc)

    for c in range(n_chunk):
        out_ref[:, :, lanes_of(par, c)] = (attended(par, c) + acc_s[c, par]).astype(bf16)
    for c in range(n_chunk):
        inner[c].wait_recv()
        outer[2 * c].wait_recv()
        outer[2 * c + 1].wait_recv()
        out_ref[:, :, lanes_of(1 - par, c)] = (
            attended(1 - par, c) + res_in[c].astype(f32)
        ).astype(bf16)

    for copy in ag + st + pt + av + pair + inner + outer:
        copy.wait_send()

    @pl.when(direct_ok)
    def _():
        for c in range(n_chunk):
            direct[c].wait_send()

    @pl.when(forward_ok)
    def _():
        for c in range(n_chunk):
            forward[c].wait_send()

    @pl.when(has_prev)
    def _():
        for c in range(n_chunk):
            to_prev[c].wait_send()

    @pl.when(has_next)
    def _():
        for c in range(n_chunk):
            to_next[c].wait_send()


def on_device_fused(queries, key_states, value_states, conv_weight):
    n_tm, n_sp = lax.axis_size("tm"), lax.axis_size("space")
    tokens = FRAMES * ROWS_DEV * COLUMNS
    lc = 4 * HEAD_DIM
    n_chunk = D // 2 // lc
    agents = AGENT_DEV * n_sp
    ha = lc // HEAD_DIM * agents
    each = HEAD_DIM // n_sp
    n_piece = 16 // AGENT_DEV
    piece = D // n_piece
    f32, bf16 = jnp.float32, jnp.bfloat16
    dma = pltpu.SemaphoreType.DMA
    side = (n_chunk, 2, COLUMNS, lc)
    whole = (n_chunk, FRAMES, COLUMNS, lc)
    vmem = pl.BlockSpec(memory_space=pltpu.VMEM)
    hbm = pl.BlockSpec(memory_space=pltpu.HBM)
    mixed = pl.pallas_call(
        functools.partial(fused, n_tm, n_sp),
        out_shape=jax.ShapeDtypeStruct((FRAMES, COLUMNS, D), bf16),
        in_specs=[hbm] * 4,
        out_specs=vmem,
        scratch_shapes=[
            pltpu.VMEM((FRAMES, COLUMNS, D), bf16),
            pltpu.VMEM((tokens, D), bf16),
            pltpu.VMEM((FRAMES, COLUMNS, D), bf16),
            pltpu.VMEM(conv_weight.shape, f32),
            pltpu.VMEM((16, piece), f32),
            pltpu.VMEM((n_sp, 16, piece), bf16),
            pltpu.VMEM((agents, D), bf16),
            pltpu.VMEM((2 * n_chunk, ha, lc), bf16),
            pltpu.VMEM((n_sp, 2 * each, n_chunk * ha), bf16),
            pltpu.VMEM((n_sp, 2 * each, n_chunk * ha), bf16),
            pltpu.VMEM((n_sp, 1, 2 * n_chunk * ha), f32),
            pltpu.VMEM((n_sp, 2 * each, n_chunk * ha), bf16),
            pltpu.VMEM((2, HEAD_DIM, n_chunk * ha), bf16),
            pltpu.VMEM((2 * n_chunk, tokens, ha), bf16),
            pltpu.VMEM((n_chunk, 4, FRAMES, COLUMNS, lc), bf16),
            pltpu.VMEM((n_chunk, 2, FRAMES, COLUMNS, lc), f32),
            pltpu.VMEM(side, bf16),
            pltpu.VMEM(side, bf16),
            pltpu.VMEM(side, bf16),
            pltpu.VMEM(side, bf16),
            pltpu.VMEM(whole, bf16),
            pltpu.VMEM(whole, bf16),
            dma((2, n_sp)),
            dma((2, n_sp)),
            dma((2, n_sp)),
            dma((2, n_sp)),
            dma((2, n_chunk)),
            dma((2, n_chunk)),
            dma((2, n_chunk)),
            dma((2, n_chunk)),
            dma((2, n_chunk)),
            dma((2, 3 * n_chunk)),
            dma((4,)),
        ],
        compiler_params=pltpu.CompilerParams(
            collective_id=0, has_side_effects=True, vmem_limit_bytes=63 * 1024 * 1024
        ),
    )(
        queries.reshape(FRAMES, COLUMNS, D),
        key_states.reshape(tokens, D),
        value_states.reshape(FRAMES, COLUMNS, D),
        conv_weight,
    )
    return mixed.reshape(value_states.shape)


def solution(mesh):
    fits = mesh.shape["space"] * 8 == HEAD_DIM
    return jax.shard_map(
        on_device_fused if fits else on_device,
        mesh=mesh,
        in_specs=(
            P("tm", None, "space", None, None),
            P("tm", None, "space", None, None),
            P("tm", None, "space", None, None),
            P(),
        ),
        out_specs=P("tm", None, "space", None, None),
        check_vma=False,
    )
```

```python
import functools
import math

import jax
import jax.numpy as jnp
from jax import lax
from jax.experimental import pallas as pl
from jax.experimental.pallas import tpu as pltpu
from jax.sharding import PartitionSpec as P

HEADS = 24
HEAD_DIM = 64
D = 1536
FRAMES = 4
ROWS_DEV = 1
COLUMNS = 32
AGENT_DEV = 4
MESH = pl.DeviceIdType.MESH


def extended(cells, sides, width):
    for axis, dim in sides:
        count = lax.axis_size(axis)
        ends = count - 1
        head = lax.slice_in_dim(cells, 0, width, axis=dim)
        tail = lax.slice_in_dim(cells, cells.shape[dim] - width, cells.shape[dim], axis=dim)
        cells = jnp.concatenate(
            [
                lax.ppermute(tail, axis, [(i, (i + 1) % count) for i in range(ends)]),
                cells,
                lax.ppermute(head, axis, [((i + 1) % count, i) for i in range(ends)]),
            ],
            axis=dim,
        )
    return cells


def merged_2(part, axis, combine):
    gathered = jax.tree.map(lambda a: lax.all_gather(a, axis), part)

    def take(source):
        return jax.tree.map(lambda a: lax.dynamic_index_in_dim(a, source, 0, False), gathered)

    return lax.fori_loop(
        1, lax.axis_size(axis), lambda source, state: combine(state, take(source)), take(0)
    )


def mix_local(window, conv_weight):
    shape = (window.shape[0] - 2, window.shape[1] - 2, window.shape[2] - 2, window.shape[3])
    total = jnp.zeros(shape, jnp.float32)
    for time_off in range(3):
        for row_off in range(3):
            for col_off in range(3):
                piece = window[
                    time_off : time_off + shape[0],
                    row_off : row_off + shape[1],
                    col_off : col_off + shape[2],
                ]
                total = total + piece.astype(jnp.float32) * conv_weight[time_off, row_off, col_off]
    return total


def pair_merge(first, second):
    peak = jnp.maximum(first[0], second[0])
    left = jnp.exp(first[0] - peak)
    right = jnp.exp(second[0] - peak)
    return (
        peak,
        first[1] * left + second[1] * right,
        first[2] * left[..., None] + second[2] * right[..., None],
    )


def on_device(queries, key_states, value_states, conv_weight):
    tokens = FRAMES * ROWS_DEV * COLUMNS
    inv_root = HEAD_DIM ** (-0.5)
    per_block = math.gcd(HEADS, 8)
    blocks = HEADS // per_block
    padded = extended(value_states, (("tm", 1), ("space", 2)), 1)
    window = jnp.pad(padded[0], ((0, 0), (0, 0), (1, 1), (0, 0)))
    pooled = jnp.mean(
        queries.reshape(FRAMES, ROWS_DEV, AGENT_DEV, COLUMNS // AGENT_DEV, D),
        axis=(0, 1, 3),
        dtype=jnp.float32,
    )
    agents = lax.all_gather(pooled.astype(jnp.bfloat16), "space", axis=0, tiled=True)
    count = agents.shape[0]
    agent_heads = agents.reshape(count, HEADS, HEAD_DIM)
    query_heads = queries.reshape(tokens, HEADS, HEAD_DIM)
    key_heads = key_states.reshape(tokens, HEADS, HEAD_DIM)
    value_heads = value_states.reshape(tokens, HEADS, HEAD_DIM)

    def agent_block(index):
        start = index * per_block
        agent_part = lax.dynamic_slice_in_dim(agent_heads, start, per_block, 1)
        key_part = lax.dynamic_slice_in_dim(key_heads, start, per_block, 1)
        value_part = lax.dynamic_slice_in_dim(value_heads, start, per_block, 1)
        scores = (
            jnp.einsum("ahd,nhd->ahn", agent_part, key_part, preferred_element_type=jnp.float32)
            * inv_root
        )
        block_peak = jnp.max(scores, axis=2)
        weights = jnp.exp(scores - block_peak[..., None])
        block_total = jnp.sum(weights, axis=2)
        block_acc = jnp.einsum(
            "ahn,nhd->ahd",
            weights.astype(jnp.bfloat16),
            value_part,
            preferred_element_type=jnp.float32,
        )
        return (block_peak, block_total, block_acc)

    peaks, totals, accs = lax.map(agent_block, jnp.arange(blocks, dtype=jnp.int32))
    local_peak = peaks.transpose(1, 0, 2).reshape(count, HEADS)
    local_total = totals.transpose(1, 0, 2).reshape(count, HEADS)
    local_acc = accs.transpose(1, 0, 2, 3).reshape(count, HEADS, HEAD_DIM)
    merged = merged_2((local_peak, local_total, local_acc), "space", pair_merge)
    agent_values = (merged[2] / merged[1][..., None]).astype(jnp.bfloat16)

    def query_block(index):
        start = index * per_block
        query_part = lax.dynamic_slice_in_dim(query_heads, start, per_block, 1)
        agent_part = lax.dynamic_slice_in_dim(agent_heads, start, per_block, 1)
        values_part = lax.dynamic_slice_in_dim(agent_values, start, per_block, 1)
        query_scores = (
            jnp.einsum("nhd,ahd->hna", query_part, agent_part, preferred_element_type=jnp.float32)
            * inv_root
        )
        probs = jax.nn.softmax(query_scores, axis=-1).astype(jnp.bfloat16)
        return jnp.einsum("hna,ahd->nhd", probs, values_part, preferred_element_type=jnp.float32)

    outputs = lax.map(query_block, jnp.arange(blocks, dtype=jnp.int32))
    attended = outputs.transpose(1, 0, 2, 3).reshape(FRAMES, ROWS_DEV, COLUMNS, D)
    local_mix = mix_local(window, conv_weight)
    mixed = (attended + local_mix).astype(jnp.bfloat16)
    return mixed.reshape(value_states.shape)


def mesh_copy(src, dst, send, recv, device):
    return pltpu.make_async_remote_copy(
        src_ref=src,
        dst_ref=dst,
        send_sem=send,
        recv_sem=recv,
        device_id=device,
        device_id_type=MESH,
    )


def fused(
    n_tm,
    n_sp,
    q_hbm,
    k_hbm,
    v_hbm,
    w_hbm,
    out_ref,
    q_ref,
    k_ref,
    v_ref,
    w_ref,
    pool_s,
    gather,
    agents_s,
    blocks_s,
    parts_out,
    parts_in,
    stats,
    av_in,
    avt_s,
    wt_s,
    rows,
    acc_s,
    prev_out,
    next_out,
    prev_in,
    next_in,
    res_out,
    res_in,
    ag_sem,
    st_sem,
    pt_sem,
    av_sem,
    pair_sem,
    side_send,
    side_recv,
    time_send,
    time_recv,
    res_sem,
    in_sem,
):
    loads = [
        pltpu.make_async_copy(source, held, in_sem.at[i])
        for i, (source, held) in enumerate(
            ((q_hbm, q_ref), (v_hbm, v_ref), (k_hbm, k_ref), (w_hbm, w_ref))
        )
    ]
    for load in loads:
        load.start()
    q_load, v_load, k_load, w_load = loads
    f32, bf16 = jnp.float32, jnp.bfloat16
    tm, me = lax.axis_index("tm"), lax.axis_index("space")
    par = lax.rem(me, 2)
    z = me // 2
    partner = me + 1 - 2 * par
    has_lo, has_hi = z > 0, z < n_sp // 2 - 1
    has_prev, has_next = tm > 0, tm < n_tm - 1
    inv_root = HEAD_DIM ** (-0.5)
    frames, cols, width = v_ref.shape
    tokens = frames * cols
    half = width // 2
    n_chunk, lc = rows.shape[0], rows.shape[4]
    n_block = n_chunk * 2
    agents = AGENT_DEV * n_sp
    per = lc // HEAD_DIM
    ha = per * agents
    piece = gather.shape[2]
    n_piece = width // piece
    lanes_half = n_chunk * ha
    nt = (((1,), (1,)), ((), ()))

    barrier = pltpu.get_barrier_semaphore()
    peers = [lax.rem(me + d, n_sp) for d in range(n_sp)]
    sources = [lax.rem(me + n_sp - d, n_sp) for d in range(n_sp)]
    for d in range(1, n_sp):
        pl.semaphore_signal(barrier, inc=1, device_id=(tm, peers[d]), device_id_type=MESH)

    @pl.when(has_prev)
    def _():
        pl.semaphore_signal(barrier, inc=1, device_id=(tm - 1, me), device_id_type=MESH)

    @pl.when(has_next)
    def _():
        pl.semaphore_signal(barrier, inc=1, device_id=(tm + 1, me), device_id_type=MESH)

    q_load.wait()
    summed = q_ref[0].astype(f32)
    for f in range(1, frames):
        summed = summed + q_ref[f].astype(f32)
    group = cols // AGENT_DEV
    for j in range(AGENT_DEV):
        mean = jnp.sum(summed[j * group : (j + 1) * group], axis=0, keepdims=True) * (
            1.0 / (frames * group)
        )
        for p in range(n_piece):
            pool_s[p * AGENT_DEV + j : p * AGENT_DEV + j + 1, :] = mean[:, p * piece : (p + 1) * piece]
    gather[me] = pool_s[...].astype(bf16)

    greeted = n_sp - 1 + jnp.where(has_prev, 1, 0) + jnp.where(has_next, 1, 0)
    pl.semaphore_wait(barrier, greeted)

    def to_all(src_of, dst, sem):
        return [
            mesh_copy(src_of(d), dst.at[me], sem.at[0, d], sem.at[1, d], (tm, peers[d]))
            for d in range(1, n_sp)
        ]

    def from_all(dst, sem):
        for d in range(1, n_sp):
            mesh_copy(
                dst.at[sources[d]], dst.at[sources[d]], sem.at[0, d], sem.at[1, d], (tm, peers[d])
            ).wait_recv()

    ag = to_all(lambda d: gather.at[me], gather, ag_sem)
    for copy in ag:
        copy.start()

    v_load.wait()

    def lanes_of(side, c):
        return pl.ds(pl.multiple_of(side * half + c * lc, lc), lc)

    pair = []
    for c in range(n_chunk):
        copy = mesh_copy(
            v_ref.at[:, :, lanes_of(1 - par, c)],
            rows.at[c, 1 + par],
            pair_sem.at[0, c],
            pair_sem.at[1, c],
            (tm, partner),
        )
        copy.start()
        pair.append(copy)

    direct_ok = jnp.where(par == 0, z, n_sp // 2 - 1 - z) > 0
    forward_ok = jnp.where(par == 0, n_sp // 2 - 1 - z, z) > 0
    direct_to = me + 4 * par - 2
    forward_to = me + 2 - 4 * par
    direct = [
        mesh_copy(
            v_ref.at[:, :, lanes_of(par, c)],
            rows.at[c, 3 - 3 * par],
            side_send.at[0, c],
            side_recv.at[1 - par, c],
            (tm, direct_to),
        )
        for c in range(n_chunk)
    ]
    forward = [
        mesh_copy(
            rows.at[c, 2 - par],
            rows.at[c, 3 * par],
            side_send.at[1, c],
            side_recv.at[par, c],
            (tm, forward_to),
        )
        for c in range(n_chunk)
    ]

    @pl.when(direct_ok)
    def _():
        for c in range(n_chunk):
            direct[c].start()

    def pass_on(c):
        mesh_copy(
            v_ref.at[:, :, lanes_of(1 - par, c)],
            rows.at[c, 2 - par],
            pair_sem.at[0, c],
            pair_sem.at[1, c],
            (tm, partner),
        ).wait_recv()

        @pl.when(forward_ok)
        def _():
            forward[c].start()

    zero_row = jnp.zeros((frames, cols, lc), bf16)
    zero_part = jnp.zeros(prev_in.shape, bf16)
    for c in range(n_chunk):
        rows[c, 1 + par] = v_ref[:, :, lanes_of(par, c)]

        @pl.when(z == 0)
        def _():
            rows[c, 0] = zero_row

        @pl.when(z == n_sp // 2 - 1)
        def _():
            rows[c, 3] = zero_row

    @pl.when(tm == 0)
    def _():
        prev_in[...] = zero_part

    @pl.when(tm == n_tm - 1)
    def _():
        next_in[...] = zero_part

    pass_on(0)
    from_all(gather, ag_sem)

    packed = gather[...].reshape(n_sp * n_piece * AGENT_DEV, piece)
    row = lax.broadcasted_iota(jnp.int32, (agents, packed.shape[0]), 0)
    col = lax.broadcasted_iota(jnp.int32, (agents, packed.shape[0]), 1)
    span = n_piece * AGENT_DEV
    for p in range(n_piece):
        wanted = (row // AGENT_DEV) * span + p * AGENT_DEV + lax.rem(row, AGENT_DEV)
        pick = jnp.where(col == wanted, 1.0, 0.0).astype(bf16)
        agents_s[:, p * piece : (p + 1) * piece] = jnp.dot(
            pick, packed, preferred_element_type=f32
        ).astype(bf16)

    ch = lax.broadcasted_iota(jnp.int32, (agents, lc), 1) // HEAD_DIM
    lane_head = lax.broadcasted_iota(jnp.int32, (HEAD_DIM, ha), 1) // agents
    for b in range(n_block):
        block = agents_s[:, b * lc : (b + 1) * lc].astype(f32)
        blocks_s[b] = jnp.concatenate(
            [jnp.where(ch == h, block, 0.0) for h in range(per)], axis=0
        ).astype(bf16)

    k_load.wait()
    compact = []
    for b in range(n_block):
        if 0 < b < n_chunk:
            pass_on(b)
        keys = k_ref[:, b * lc : (b + 1) * lc]
        scores = lax.dot_general(keys, blocks_s[b], nt, preferred_element_type=f32) * inv_root
        peak = jnp.max(scores, axis=0, keepdims=True)
        weights = jnp.exp(scores - peak)
        at = slice(b * ha, (b + 1) * ha)
        sums = jnp.sum(weights, axis=0, keepdims=True)
        stats[me, 0:1, at] = peak + jnp.log(sums)
        values = v_ref[:, :, b * lc : (b + 1) * lc].reshape(tokens, lc)
        full = lax.dot_general(
            values, weights.astype(bf16), (((0,), (0,)), ((), ())), preferred_element_type=f32
        )
        small = jnp.where(lane_head == 0, full[0:HEAD_DIM], 0.0)
        for h in range(1, per):
            small = jnp.where(lane_head == h, full[h * HEAD_DIM : (h + 1) * HEAD_DIM], small)
        compact.append(small / sums)
    st = to_all(lambda d: stats.at[me], stats, st_sem)
    for copy in st:
        copy.start()
    low = jnp.concatenate(compact[:n_chunk], axis=1)
    high = jnp.concatenate(compact[n_chunk:], axis=1)
    each = HEAD_DIM // n_sp
    for s in range(n_sp):
        at = slice(s * each, (s + 1) * each)
        parts_out[s] = jnp.concatenate([low[at], high[at]], axis=0).astype(bf16)
    pt = to_all(lambda d: parts_out.at[peers[d]], parts_in, pt_sem)
    for copy in pt:
        copy.start()
    parts_in[me] = parts_out[me]

    for b in range(n_block):
        asked = q_ref[:, :, b * lc : (b + 1) * lc].reshape(tokens, lc)
        scores = lax.dot_general(blocks_s[b], asked, nt, preferred_element_type=f32) * inv_root
        scores = scores.reshape(per, agents, tokens)
        raised = jnp.exp(scores - jnp.max(scores, axis=1, keepdims=True))
        probs = raised / jnp.sum(raised, axis=1, keepdims=True)
        wt_s[b] = probs.reshape(ha, tokens).T.astype(bf16)

    column = lax.broadcasted_iota(jnp.int32, (cols, 128), 0)

    def convolve(c):
        @pl.when(has_lo)
        def _():
            mesh_copy(
                rows.at[c, 0], rows.at[c, 0], side_send.at[0, c], side_recv.at[0, c], (tm, partner)
            ).wait_recv()

        @pl.when(has_hi)
        def _():
            mesh_copy(
                rows.at[c, 3], rows.at[c, 3], side_send.at[0, c], side_recv.at[1, c], (tm, partner)
            ).wait_recv()

        def tile(step, carry):
            o, sub = step // (lc // 128), lax.rem(step, lc // 128)
            at = pl.ds(pl.multiple_of(sub * 128, 128), 128)
            w_at = pl.ds(pl.multiple_of(par * half + c * lc + sub * 128, 128), 128)
            for out_f in range(-1, frames + 1):
                sums = [None, None, None]
                for i in range(3):
                    f = out_f + i - 1
                    if f < 0 or f >= frames:
                        continue
                    for j in range(3):
                        x = rows[c, o + j, f, :, at].astype(f32)
                        for k in range(3):
                            term = x * w_ref[i, j, k : k + 1, w_at]
                            sums[k] = term if sums[k] is None else sums[k] + term
                before = jnp.where(column == 0, 0.0, pltpu.roll(sums[0], 1, 0))
                after = jnp.where(column == cols - 1, 0.0, pltpu.roll(sums[2], cols - 1, 0))
                total = sums[1] + before + after
                if out_f < 0:
                    prev_out[c, o, :, at] = total.astype(bf16)
                elif out_f == frames:
                    next_out[c, o, :, at] = total.astype(bf16)
                else:
                    acc_s[c, o, out_f, :, at] = total
            return carry

        lax.fori_loop(0, 2 * (lc // 128), tile, 0)

        @pl.when(has_prev)
        def _():
            to_prev[c].start()

        @pl.when(has_next)
        def _():
            to_next[c].start()

        res_out[c, 1:last] = acc_s[c, 1 - par, 1:last].astype(bf16)
        inner[c].start()

    to_prev = [
        mesh_copy(
            prev_out.at[c], next_in.at[c], time_send.at[0, c], time_recv.at[0, c], (tm - 1, me)
        )
        for c in range(n_chunk)
    ]
    to_next = [
        mesh_copy(
            next_out.at[c], prev_in.at[c], time_send.at[1, c], time_recv.at[1, c], (tm + 1, me)
        )
        for c in range(n_chunk)
    ]
    last = frames - 1
    inner = [
        mesh_copy(
            res_out.at[c, 1:last],
            res_in.at[c, 1:last],
            res_sem.at[0, c],
            res_sem.at[1, c],
            (tm, partner),
        )
        for c in range(n_chunk)
    ]
    outer = [
        mesh_copy(
            res_out.at[c, f],
            res_in.at[c, f],
            res_sem.at[0, (e + 1) * n_chunk + c],
            res_sem.at[1, (e + 1) * n_chunk + c],
            (tm, partner),
        )
        for c in range(n_chunk)
        for e, f in enumerate((0, last))
    ]

    def finish(c):
        @pl.when(has_prev)
        def _():
            to_next[c].wait_recv()

        @pl.when(has_next)
        def _():
            to_prev[c].wait_recv()

        for o in range(2):
            acc_s[c, o, 0] += prev_in[c, o].astype(f32)
            acc_s[c, o, frames - 1] += next_in[c, o].astype(f32)
        for e, f in enumerate((0, last)):
            res_out[c, f] = acc_s[c, 1 - par, f].astype(bf16)
            outer[2 * c + e].start()

    w_load.wait()
    for c in range(n_chunk):
        convolve(c)
        if c > 0:
            finish(c - 1)

    from_all(stats, st_sem)
    from_all(parts_in, pt_sem)
    peaks = stats[...]
    top = jnp.max(peaks, axis=0)
    total = jnp.zeros_like(top)
    merged = [jnp.zeros((each, lanes_half), f32) for _ in range(2)]
    for s in range(n_sp):
        scale = jnp.exp(peaks[s] - top)
        total = total + scale
        part = parts_in[s].astype(f32)
        for g in range(2):
            merged[g] = merged[g] + part[g * each : (g + 1) * each] * scale[
                :, g * lanes_half : (g + 1) * lanes_half
            ]
    av_in[me] = jnp.concatenate(
        [merged[g] / total[:, g * lanes_half : (g + 1) * lanes_half] for g in range(2)], axis=0
    ).astype(bf16)
    av = to_all(lambda d: av_in.at[me], av_in, av_sem)
    for copy in av:
        copy.start()

    finish(n_chunk - 1)

    from_all(av_in, av_sem)
    spread = av_in[...].astype(f32)
    for g in range(2):
        avt_s[g] = (
            spread[:, g * each : (g + 1) * each, :].reshape(HEAD_DIM, lanes_half).astype(bf16)
        )

    def attended(side, c):
        small = avt_s[side, :, c * ha : (c + 1) * ha].astype(f32)
        spread_values = jnp.concatenate(
            [jnp.where(lane_head == h, small, 0.0) for h in range(per)], axis=0
        ).astype(bf16)
        got = lax.dot_general(
            wt_s[side * n_chunk + c], spread_values, nt, preferred_element_type=f32
        )
        return got.reshape(frames, cols, lc)

    for c in range(n_chunk):
        out_ref[:, :, lanes_of(par, c)] = (attended(par, c) + acc_s[c, par]).astype(bf16)
    for c in range(n_chunk):
        inner[c].wait_recv()
        outer[2 * c].wait_recv()
        outer[2 * c + 1].wait_recv()
        out_ref[:, :, lanes_of(1 - par, c)] = (
            attended(1 - par, c) + res_in[c].astype(f32)
        ).astype(bf16)

    for copy in ag + st + pt + av + pair + inner + outer:
        copy.wait_send()

    @pl.when(direct_ok)
    def _():
        for c in range(n_chunk):
            direct[c].wait_send()

    @pl.when(forward_ok)
    def _():
        for c in range(n_chunk):
            forward[c].wait_send()

    @pl.when(has_prev)
    def _():
        for c in range(n_chunk):
            to_prev[c].wait_send()

    @pl.when(has_next)
    def _():
        for c in range(n_chunk):
            to_next[c].wait_send()


def on_device_fused(queries, key_states, value_states, conv_weight):
    n_tm, n_sp = lax.axis_size("tm"), lax.axis_size("space")
    tokens = FRAMES * ROWS_DEV * COLUMNS
    lc = 4 * HEAD_DIM
    n_chunk = D // 2 // lc
    agents = AGENT_DEV * n_sp
    ha = lc // HEAD_DIM * agents
    each = HEAD_DIM // n_sp
    n_piece = 16 // AGENT_DEV
    piece = D // n_piece
    f32, bf16 = jnp.float32, jnp.bfloat16
    dma = pltpu.SemaphoreType.DMA
    side = (n_chunk, 2, COLUMNS, lc)
    whole = (n_chunk, FRAMES, COLUMNS, lc)
    vmem = pl.BlockSpec(memory_space=pltpu.VMEM)
    hbm = pl.BlockSpec(memory_space=pltpu.HBM)
    mixed = pl.pallas_call(
        functools.partial(fused, n_tm, n_sp),
        out_shape=jax.ShapeDtypeStruct((FRAMES, COLUMNS, D), bf16),
        in_specs=[hbm] * 4,
        out_specs=vmem,
        scratch_shapes=[
            pltpu.VMEM((FRAMES, COLUMNS, D), bf16),
            pltpu.VMEM((tokens, D), bf16),
            pltpu.VMEM((FRAMES, COLUMNS, D), bf16),
            pltpu.VMEM(conv_weight.shape, f32),
            pltpu.VMEM((16, piece), f32),
            pltpu.VMEM((n_sp, 16, piece), bf16),
            pltpu.VMEM((agents, D), bf16),
            pltpu.VMEM((2 * n_chunk, ha, lc), bf16),
            pltpu.VMEM((n_sp, 2 * each, n_chunk * ha), bf16),
            pltpu.VMEM((n_sp, 2 * each, n_chunk * ha), bf16),
            pltpu.VMEM((n_sp, 1, 2 * n_chunk * ha), f32),
            pltpu.VMEM((n_sp, 2 * each, n_chunk * ha), bf16),
            pltpu.VMEM((2, HEAD_DIM, n_chunk * ha), bf16),
            pltpu.VMEM((2 * n_chunk, tokens, ha), bf16),
            pltpu.VMEM((n_chunk, 4, FRAMES, COLUMNS, lc), bf16),
            pltpu.VMEM((n_chunk, 2, FRAMES, COLUMNS, lc), f32),
            pltpu.VMEM(side, bf16),
            pltpu.VMEM(side, bf16),
            pltpu.VMEM(side, bf16),
            pltpu.VMEM(side, bf16),
            pltpu.VMEM(whole, bf16),
            pltpu.VMEM(whole, bf16),
            dma((2, n_sp)),
            dma((2, n_sp)),
            dma((2, n_sp)),
            dma((2, n_sp)),
            dma((2, n_chunk)),
            dma((2, n_chunk)),
            dma((2, n_chunk)),
            dma((2, n_chunk)),
            dma((2, n_chunk)),
            dma((2, 3 * n_chunk)),
            dma((4,)),
        ],
        compiler_params=pltpu.CompilerParams(
            collective_id=0, has_side_effects=True, vmem_limit_bytes=63 * 1024 * 1024
        ),
    )(
        queries.reshape(FRAMES, COLUMNS, D),
        key_states.reshape(tokens, D),
        value_states.reshape(FRAMES, COLUMNS, D),
        conv_weight,
    )
    return mixed.reshape(value_states.shape)


def solution(mesh):
    fits = mesh.shape["space"] * 8 == HEAD_DIM
    return jax.shard_map(
        on_device_fused if fits else on_device,
        mesh=mesh,
        in_specs=(
            P("tm", None, "space", None, None),
            P("tm", None, "space", None, None),
            P("tm", None, "space", None, None),
            P(),
        ),
        out_specs=P("tm", None, "space", None, None),
        check_vma=False,
    )
```
